32 devices in a mesh: path: 4 (over y, core), fsdp: 8 (over z, x).
Axes of the slice: x: 2, y: 2, z: 4, core: 2. Of those that a mesh axis runs over, the one named last changes fastest.
Arguments:
- inputs: bfloat16 [4, 1024, 2048], P('path', 'fsdp'), may hold values from -6 to 6
- targets: bfloat16 [4, 1024, 2048], P('path', 'fsdp'), may hold values from -6 to 6
- token_ids: int32 [4, 1024], P('path', 'fsdp'), may hold values from 0 to 31999, as said below
- module_table: int32 [4, 2], replicated, may hold values from 0 to 3, as said below
- path_weights: bfloat16 [4, 2, 2048, 5632], P('path', None, None, 'fsdp'), may hold values from -6 to 6
- master: float32 [2, 4, 2048, 5632], P(None, None, 'path', 'fsdp'), may hold values from -6 to 6
- momentum: float32 [2, 4, 2048, 5632], P(None, None, 'path', 'fsdp'), may hold values from -6 to 6
Outputs:
- new_weights: bfloat16 [4, 2, 2048, 5632], P('path', None, None, 'fsdp')
- new_master: float32 [2, 4, 2048, 5632], P(None, None, 'path', 'fsdp')
- new_momentum: float32 [2, 4, 2048, 5632], P(None, None, 'path', 'fsdp')
The draws below stay inside these ranges and needn't reach their ends.
Inputs may be any that keep to these rules, and one draw needn't show every extreme that they name: `module_table`: at each level, every module is named by exactly 1 paths. `token_ids`: ids below 256 are control tokens.
All inputs are finite; a program needn't handle non-finite values.
Results may differ from the reference program's by a relative error of at most 0.014.
Values may be sent and summed in bfloat16 or wider, within the bound.
No kernel may reach another device: no remote copies, remote signals or barrier semaphores. Data moves between devices by JAX's collectives and lax.ppermute only.
A program may use at most 128 MiB of HBM per device.

```python
import jax
import jax.numpy as jnp
from jax import lax

D = 2048
FF = 5632
VOCAB = 32000
SPECIAL = 256
MODS = 4
LEVELS = 2
PATHS = 4
TOKENS = 1024
N_FSDP = 8


def draw_token_ids(key, part):
    key = jax.random.fold_in(key, 11)
    k_kind, k_control, k_text, k_spots = jax.random.split(key, 4)
    kind = jax.random.randint(k_kind, (PATHS, TOKENS), 0, 3)
    control = jax.random.randint(k_control, (PATHS, TOKENS), 0, SPECIAL)
    text = jax.random.randint(k_text, (PATHS, TOKENS), SPECIAL, VOCAB)
    drawn = jnp.where(kind == 0, control, text)
    spots = jax.random.randint(k_spots, (2,), 0, PATHS * TOKENS)
    flat_pos = jnp.arange(PATHS * TOKENS, dtype=jnp.int32).reshape(PATHS, TOKENS)
    drawn = jnp.where(flat_pos == spots[0], VOCAB - 1, drawn)
    drawn = jnp.where(flat_pos == spots[1], 0, drawn)
    return drawn.astype(jnp.int32)


def draw_module_table(key, part):
    key = jax.random.fold_in(key, 23)
    columns = []
    for level in range(LEVELS):
        order = jax.random.permutation(jax.random.fold_in(key, level), PATHS)
        columns.append(order % MODS)
    return jnp.stack(columns, axis=1).astype(jnp.int32)


def level_of(rng, extent, cuts, smallest, largest):
    factor_of, own = 1.0, jax.random.fold_in(rng, 6)
    for dim, parts in cuts:
        draws = jnp.exp(jax.random.uniform(jax.random.fold_in(own, dim), (parts,), jnp.float32, smallest / len(cuts), largest / len(cuts)))
        factor_of = factor_of * jnp.repeat(draws, extent[dim] // parts).reshape([-1 if axis == dim else 1 for axis in range(len(extent))])
    return factor_of


def normal_values(own_key, shape, scale, bound, cuts=(), kind=jnp.bfloat16):
    result = scale * jax.random.normal(own_key, shape, jnp.float32)
    if cuts:
        result = result * level_of(own_key, shape, cuts, -0.22, 0.18)
    return jnp.clip(result, -bound, bound).astype(kind)


def setup_inputs(seed: int = 0) -> dict:
    splits = jax.random.split(jax.random.key(seed), 8)
    return {
        "inputs": normal_values(splits[0], (PATHS, TOKENS, D), 1.0, 6.0, ((0, 4), (1, 8))),
        "targets": normal_values(splits[1], (PATHS, TOKENS, D), 1.0, 6.0, ((0, 4), (1, 8))),
        "token_ids": draw_token_ids(jax.random.fold_in(splits[7], 71), 0),
        "module_table": draw_module_table(jax.random.fold_in(splits[7], 71), 0),
        "path_weights": normal_values(splits[4], (PATHS, LEVELS, D, FF), 1.0, 6.0, ((0, 4), (3, 8))),
        "master": normal_values(splits[5], (LEVELS, MODS, D, FF), 1.0, 6.0, ((2, 4), (3, 8)), jnp.float32),
        "momentum": normal_values(splits[6], (LEVELS, MODS, D, FF), 1.0, 6.0, ((2, 4), (3, 8)), jnp.float32),
    }


INNER_LR = 4096.0
OUTER_LR = 0.7
MOMENT = 0.9


def path_delta(x_rows, tgt_rows, ids, w_in, w_out):
    piece = FF // N_FSDP
    pre = jnp.dot(x_rows, w_in, preferred_element_type=jnp.float32) * (D ** -0.5)
    sig = jax.nn.sigmoid(pre)
    act = (pre * sig).astype(jnp.bfloat16)

    def add_block(total, block):
        start = (block * piece).astype(jnp.int32)
        a_part = lax.dynamic_slice_in_dim(act, start, piece, 1)
        w_part = lax.dynamic_slice_in_dim(w_out, start, piece, 1)
        term = lax.dot_general(a_part, w_part, (((1,), (1,)), ((), ())), preferred_element_type=jnp.float32) * (FF ** -0.5)
        rounded = lax.optimization_barrier(term.astype(jnp.bfloat16))
        return total + rounded.astype(jnp.float32), None

    mixed, _ = lax.scan(add_block, jnp.zeros((TOKENS, D), jnp.float32), jnp.arange(N_FSDP, dtype=jnp.int32))
    keep = (ids >= SPECIAL).astype(jnp.float32)
    out_grad = (keep[:, None] * (x_rows.astype(jnp.float32) + mixed - tgt_rows.astype(jnp.float32)) / TOKENS).astype(jnp.bfloat16)
    act_grad = jnp.dot(out_grad, w_out, preferred_element_type=jnp.float32) * (FF ** -0.5)
    pre_grad = (act_grad * sig * (1.0 + pre * (1.0 - sig))).astype(jnp.bfloat16)
    grad_out = lax.dot_general(out_grad, act, (((0,), (0,)), ((), ())), preferred_element_type=jnp.float32) * (FF ** -0.5)
    grad_in = lax.dot_general(x_rows, pre_grad, (((0,), (0,)), ((), ())), preferred_element_type=jnp.float32) * (D ** -0.5)
    return jnp.stack([INNER_LR * grad_in, INNER_LR * grad_out])


def reference(inputs, targets, token_ids, module_table, path_weights, master, momentum):
    labels = jnp.arange(MODS, dtype=jnp.int32)

    def add_path(sums, index):
        delta = path_delta(inputs[index], targets[index], token_ids[index], path_weights[index, 0], path_weights[index, 1])
        pick = (module_table[index][:, None] == labels[None, :]).astype(jnp.float32)
        return sums + pick[:, :, None, None] * delta[:, None], None

    sums, _ = lax.scan(add_path, jnp.zeros((LEVELS, MODS, D, FF), jnp.float32), jnp.arange(PATHS, dtype=jnp.int32))
    counts = jnp.sum((module_table.T[:, :, None] == labels[None, None, :]).astype(jnp.float32), axis=1)
    average = sums / counts[:, :, None, None]
    new_momentum = MOMENT * momentum + average
    new_master = master - OUTER_LR * (average + MOMENT * new_momentum)
    fresh = new_master.astype(jnp.bfloat16)
    levels = [jnp.take(fresh[level], module_table[:, level], axis=0) for level in range(LEVELS)]
    new_weights = jnp.stack(levels, axis=1)
    return new_weights, new_master, new_momentum
```

```python
import jax
import jax.numpy as jnp
from jax import lax
from jax.experimental import pallas as pl
from jax.experimental.pallas import tpu as pltpu
from jax.sharding import PartitionSpec as P

SPECIAL = 256


INNER_LR = 4096.0
OUTER_LR = 0.7
MOMENT = 0.9


def any_table(inputs, targets, token_ids, module_table, path_weights, master, momentum):
    x_local = inputs[0]
    w_in = path_weights[0, 0]
    w_out = path_weights[0, 1]
    width = w_in.shape[0]
    hidden_all = w_in.shape[1] * lax.axis_size("fsdp")
    out_scale = hidden_all ** (-0.5)
    x_full = lax.all_gather(x_local, "fsdp", axis=0, tiled=True)
    total = x_full.shape[0]
    pre = jnp.dot(x_full, w_in, preferred_element_type=jnp.float32) * width ** (-0.5)
    sig = jax.nn.sigmoid(pre)
    act = (pre * sig).astype(jnp.bfloat16)
    rows = act
    mine = lax.psum_scatter(
        (
            lax.dot_general(
                rows, w_out, (((1,), (1,)), ((), ())), preferred_element_type=jnp.float32
            )
            * out_scale
        ).astype(jnp.bfloat16),
        "fsdp",
        scatter_dimension=0,
        tiled=True,
    ).astype(jnp.float32)
    keep = (token_ids[0] >= SPECIAL).astype(jnp.float32)
    residual = x_local.astype(jnp.float32) + mine - targets[0].astype(jnp.float32)
    grad_mine = (keep[:, None] * residual / total).astype(jnp.bfloat16)
    piece = lax.all_gather(grad_mine, "fsdp", axis=0, tiled=True)
    rows = jnp.dot(piece, w_out, preferred_element_type=jnp.float32) * out_scale
    weight_acc = lax.dot_general(
        piece, act, (((0,), (0,)), ((), ())), preferred_element_type=jnp.float32
    )
    grad_out = weight_acc * out_scale
    pre_grad = (rows * sig * (1.0 + pre * (1.0 - sig))).astype(jnp.bfloat16)
    delta_out = INNER_LR * grad_out
    grad_in = lax.dot_general(
        x_full, pre_grad, (((0,), (0,)), ((), ())), preferred_element_type=jnp.float32
    ) * width ** (-0.5)
    stacked = jnp.stack([INNER_LR * grad_in, delta_out])[:, None]
    arrived = lax.all_to_all(
        stacked.astype(jnp.bfloat16), "path", split_axis=2, concat_axis=1, tiled=True
    ).astype(stacked.dtype)
    modules = master.shape[1]
    labels = jnp.arange(modules, dtype=jnp.int32)
    pick = (module_table.T[:, None, :] == labels[None, :, None]).astype(jnp.float32)
    counts = jnp.sum(pick, axis=2)
    sums = jnp.einsum("lmq,lqrc->lmrc", pick, arrived, precision=lax.Precision.HIGHEST)
    average = sums / counts[:, :, None, None]
    new_momentum = MOMENT * momentum + average
    new_master = master - OUTER_LR * (average + MOMENT * new_momentum)
    route = jnp.transpose(pick, (0, 2, 1)).astype(jnp.bfloat16)
    outgoing = jnp.einsum(
        "lqm,lmrc->lqrc", route, new_master.astype(jnp.bfloat16), preferred_element_type=jnp.float32
    ).astype(jnp.bfloat16)
    returned = lax.all_to_all(outgoing, "path", split_axis=1, concat_axis=2, tiled=True)
    new_weights = jnp.transpose(returned, (1, 0, 2, 3))
    return (new_weights, new_master, new_momentum)


MIB = 1024 * 1024
LANES = 1024
F32, BF16 = jnp.float32, jnp.bfloat16
NT = (((1,), (1,)), ((), ()))


def params(steps, room):
    return pltpu.CompilerParams(
        vmem_limit_bytes=room * MIB, dimension_semantics=("arbitrary",) * steps
    )


def cost(flops, moved):
    return pl.CostEstimate(flops=1, bytes_accessed=1, transcendentals=0)


def whole(shape):
    return pl.BlockSpec(shape, lambda *_: (0,) * len(shape))


def forward(pieces, weights, in_scale, out_scale, types, after):
    half, width = pieces[0].shape
    hidden = weights.shape[2]
    n, tokens = len(pieces), len(pieces) * half
    tiles = width // LANES

    def kernel(*refs):
        w_in, w_out = refs[n : n + 2]
        act_ref, slope_ref, *parts, pre_ref, flat_ref = refs[n + 2 + len(after) :]
        step = pl.program_id(0)

        @pl.when(step < tiles)
        def _():
            x = jnp.concatenate([ref[...] for ref in refs[:n]], axis=0)
            part = lax.dot_general(w_in[0, 0], x, NT, preferred_element_type=F32)

            @pl.when(step == 0)
            def _():
                pre_ref[...] = part

            @pl.when(step > 0)
            def _():
                pre_ref[...] += part

        @pl.when(step == tiles - 1)
        def _():
            pre = pre_ref[...] * in_scale
            sig = jax.nn.sigmoid(pre)
            act = pre * sig
            act_ref[...] = act.astype(BF16)
            flat_ref[...] = act.T.astype(BF16)
            slope_ref[...] = sig * (1.0 + pre * (1.0 - sig))

        @pl.when(step >= tiles)
        def _():
            part = jnp.dot(flat_ref[...], w_out[0, 0], preferred_element_type=F32) * out_scale
            for k, ref in enumerate(parts):
                ref[...] = part[k * half : (k + 1) * half].astype(ref.dtype)

    first = lambda i: (0, jnp.minimum(i, tiles - 1))
    last = lambda i: (0, jnp.maximum(i - tiles, 0))
    return pl.pallas_call(
        kernel,
        grid=(2 * tiles,),
        in_specs=[
            *[pl.BlockSpec((half, LANES), first)] * n,
            pl.BlockSpec((1, 1, hidden, LANES), lambda i: (0, 0) + first(i)),
            pl.BlockSpec((1, 1, hidden, LANES), lambda i: (0, 1) + last(i)),
        ]
        + [pl.BlockSpec(memory_space=pl.ANY)] * len(after),
        out_specs=[
            whole((hidden, tokens)),
            whole((hidden, tokens)),
            *[pl.BlockSpec((half, LANES), last)] * n,
        ],
        out_shape=[
            jax.ShapeDtypeStruct((hidden, tokens), BF16),
            jax.ShapeDtypeStruct((hidden, tokens), F32),
            *[jax.ShapeDtypeStruct((half, width), kind) for kind in types],
        ],
        scratch_shapes=[pltpu.VMEM((hidden, tokens), F32), pltpu.VMEM((tokens, hidden), BF16)],
        compiler_params=params(1, 18),
        cost_estimate=cost(4 * tokens * width * hidden, 4 * width * hidden + 10 * tokens * width),
        name="forward",
    )(*pieces, weights, weights, *after)


def backward(pieces, weights, slope, out_scale, after):
    half, width = pieces[0].shape
    hidden, tokens = slope.shape
    n = len(pieces)
    tiles = width // LANES

    def kernel(*refs):
        w_out, slope_ref = refs[n : n + 2]
        out_ref, sum_ref = refs[n + 2 + len(after) :]
        step = pl.program_id(0)
        g = jnp.concatenate([ref[...] for ref in refs[:n]], axis=0)
        part = lax.dot_general(w_out[0, 0], g, NT, preferred_element_type=F32)

        @pl.when(step == 0)
        def _():
            sum_ref[...] = part

        @pl.when(step > 0)
        def _():
            sum_ref[...] += part

        @pl.when(step == tiles - 1)
        def _():
            out_ref[...] = (sum_ref[...] * out_scale * slope_ref[...]).astype(BF16)

    return pl.pallas_call(
        kernel,
        grid=(tiles,),
        in_specs=[
            *[pl.BlockSpec((half, LANES), lambda i: (0, i))] * n,
            pl.BlockSpec((1, 1, hidden, LANES), lambda i: (0, 1, 0, i)),
            whole((hidden, tokens)),
        ]
        + [pl.BlockSpec(memory_space=pl.ANY)] * len(after),
        out_specs=whole((hidden, tokens)),
        out_shape=jax.ShapeDtypeStruct((hidden, tokens), BF16),
        scratch_shapes=[pltpu.VMEM((hidden, tokens), F32)],
        compiler_params=params(1, 12),
        cost_estimate=cost(2 * tokens * width * hidden, 2 * width * hidden + 2 * tokens * width),
        name="backward",
    )(*pieces, weights, slope, *after)


def untouched(arrays):
    return [pl.BlockSpec(memory_space=pl.ANY)] * len(arrays)


def add_rows(a, b):
    def kernel(a_ref, b_ref, out_ref):
        out_ref[...] = (a_ref[...].astype(F32) + b_ref[...].astype(F32)).astype(out_ref.dtype)

    return pl.pallas_call(
        kernel,
        out_shape=jax.ShapeDtypeStruct(a.shape, a.dtype),
        compiler_params=pltpu.CompilerParams(vmem_limit_bytes=4 * MIB),
        cost_estimate=cost(a.size, 6 * a.size),
        name="add_rows",
    )(a, b)


def base_rows(where, master, momentum, d, together, after):
    levels, _, hidden, block = master.shape

    def kernel(_, master_ref, momentum_ref, *refs):
        value = master_ref[0, 0] - (OUTER_LR * MOMENT * MOMENT) * momentum_ref[0, 0]
        outs = refs[len(after) :]
        if together:
            outs[0][0] = value.astype(BF16)
            return
        for level, out_ref in enumerate(outs):

            @pl.when(pl.program_id(0) == level)
            def _(out_ref=out_ref):
                out_ref[...] = value.astype(BF16)

    source = pl.BlockSpec(
        (1, 1, hidden, block), lambda l, s: (l, s[1 + (s[0] ^ d) * levels + l], 0, 0)
    )
    return pl.pallas_call(
        kernel,
        grid_spec=pltpu.PrefetchScalarGridSpec(
            num_scalar_prefetch=1,
            grid=(levels,),
            in_specs=[source, source] + untouched(after),
            out_specs=[pl.BlockSpec((1, hidden, block), lambda l, s: (l, 0, 0))]
            if together
            else [whole((hidden, block))] * levels,
        ),
        out_shape=[jax.ShapeDtypeStruct((levels, hidden, block), BF16)]
        if together
        else [jax.ShapeDtypeStruct((hidden, block), BF16)] * levels,
        compiler_params=params(1, 42),
        cost_estimate=cost(3 * levels * hidden * block, 10 * levels * hidden * block),
        name="base_rows",
    )(where, master, momentum, *after)


def module_rows(
    where, level, d, scale, lefts, rights, block, send=False, base=None, fresh=None, copy_shape=None, outer=None, after=()
):
    rows, wide = rights[0].shape
    hidden, tokens = lefts[0].shape
    tile = hidden
    n_left, n_right = len(lefts), len(rights)
    operands = [*lefts, *rights]
    in_specs = [pl.BlockSpec((tile, tokens), lambda i, s: (i, 0))] * n_left
    in_specs += [pl.BlockSpec((rows, block), lambda i, s: (0, s[0] ^ d if wide > block else 0))] * n_right
    out_specs, out_shape, aliases = [], [], {}
    if send:
        out_specs.append(pl.BlockSpec((tile, block), lambda i, s: (i, 0)))
        out_shape.append(jax.ShapeDtypeStruct((hidden, block), BF16))
    if base is not None:
        operands.append(base)
        if base.ndim == 3:
            in_specs.append(pl.BlockSpec((1, tile, block), lambda i, s: (level, i, 0)))
        else:
            in_specs.append(pl.BlockSpec((tile, block), lambda i, s: (i, 0)))
    if copy_shape is not None:
        if fresh is not None:
            operands.append(fresh)
            in_specs += untouched([fresh])
            aliases[len(operands)] = len(out_shape)
        out_specs.append(pl.BlockSpec((1, 1, tile, block), lambda i, s: (0, level, i, s[0] ^ d)))
        out_shape.append(jax.ShapeDtypeStruct(copy_shape, BF16))
    if outer is not None:
        master, momentum, *state = outer
        levels = master.shape[0]
        place = pl.BlockSpec(
            (1, 1, tile, block), lambda i, s: (level, s[1 + (s[0] ^ d) * levels + level], i, 0)
        )
        operands += [master, momentum, *state]
        in_specs += [place, place] + untouched(state)
        for k in range(len(state)):
            aliases[len(operands) - 1 + k] = len(out_shape) + k
        out_specs += [place, place]
        out_shape += [jax.ShapeDtypeStruct(master.shape, F32)] * 2
    n_in = len(operands) + len(after)

    def kernel(_, *refs):
        ins, outs = list(refs[:n_in]), list(refs[n_in:])
        left = jnp.concatenate([ref[...] for ref in ins[:n_left]], axis=1)
        right = jnp.concatenate([ref[...] for ref in ins[n_left : n_left + n_right]], axis=0)
        rest = ins[n_left + n_right :]
        delta = jnp.dot(left, right, preferred_element_type=F32) * scale
        if send:
            outs.pop(0)[...] = delta.astype(BF16)
        if base is not None:
            start = rest.pop(0)[...].astype(F32).reshape(tile, block)
            outs.pop(0)[0, 0] = (start - (OUTER_LR * (1.0 + MOMENT)) * delta).astype(BF16)
        if fresh is not None:
            rest.pop(0)
        if outer is not None:
            nesterov(delta, *rest[:2], *outs[-2:])
            if copy_shape is not None:
                outs[0][0, 0] = outs[-2][0, 0].astype(BF16)

    return pl.pallas_call(
        kernel,
        grid_spec=pltpu.PrefetchScalarGridSpec(
            num_scalar_prefetch=1,
            grid=(hidden // tile,),
            in_specs=in_specs + untouched(after),
            out_specs=out_specs,
        ),
        out_shape=out_shape,
        input_output_aliases=aliases,
        compiler_params=params(1, 24 if outer is None else 48),
        cost_estimate=cost(2 * hidden * block * rows * n_right, 2 * rows * n_right * (hidden + block)),
        name="module_rows",
    )(where, *operands, *after)


def nesterov(average, master_ref, momentum_ref, new_master, new_momentum):
    moved = MOMENT * momentum_ref[0, 0] + average
    new_momentum[0, 0] = moved
    new_master[0, 0] = master_ref[0, 0] - OUTER_LR * (average + MOMENT * moved)


def outer_rows(where, delta, level, d, outer):
    master, momentum, *state = outer
    levels, _, hidden, block = master.shape
    tile = hidden // 2

    def kernel(_, delta_ref, master_ref, momentum_ref, *refs):
        nesterov(delta_ref[...].astype(F32), master_ref, momentum_ref, *refs[-2:])

    place = pl.BlockSpec(
        (1, 1, tile, block), lambda i, s: (level, s[1 + (s[0] ^ d) * levels + level], i, 0)
    )
    return pl.pallas_call(
        kernel,
        grid_spec=pltpu.PrefetchScalarGridSpec(
            num_scalar_prefetch=1,
            grid=(hidden // tile,),
            in_specs=[pl.BlockSpec((tile, block), lambda i, s: (i, 0)), place, place]
            + untouched(state),
            out_specs=[place, place],
        ),
        out_shape=[jax.ShapeDtypeStruct(master.shape, F32)] * 2,
        input_output_aliases={4: 0, 5: 1} if state else {},
        compiler_params=params(1, 48),
        cost_estimate=cost(6 * hidden * block, 18 * hidden * block),
        name="outer_rows",
    )(where, delta, master, momentum, *state)


def one_path_per_module(inputs, targets, token_ids, module_table, path_weights, master, momentum):
    n_path, n_fsdp = lax.axis_size("path"), lax.axis_size("fsdp")
    steps = n_fsdp // 2
    weights = jnp.swapaxes(path_weights, 2, 3)
    master = jnp.swapaxes(master, 2, 3)
    momentum = jnp.swapaxes(momentum, 2, 3)
    width, hidden = path_weights.shape[2:]
    in_scale = width ** (-0.5)
    out_scale = (hidden * n_fsdp) ** (-0.5)
    total = inputs.shape[1] * n_fsdp

    def ring(a):
        return lax.ppermute(a, "fsdp", [(i, (i + 2) % n_fsdp) for i in range(n_fsdp)])

    def swap(a):
        return lax.ppermute(a, "fsdp", [(i, i ^ 1) for i in range(n_fsdp)])

    def cross(a, d):
        return lax.ppermute(a, "path", [(i, i ^ d) for i in range(n_path)])

    half = inputs.shape[1] // 2

    def gather(halves, use, made):
        near, far = [halves], []
        for k in range(steps - 1):
            got, came = [], []
            for h in (0, 1):
                got.append(ring(near[k][h]))
                came.append(swap(near[k][h]))
            if k:
                made = use(k - 1, [*near[k - 1], *far[k - 1]])
            for h in (0, 1):
                got[h], came[h], *_ = lax.optimization_barrier((got[h], came[h], *made))
            near.append(got)
            far.append(came)
        came = [swap(near[-1][0]), ring(far[-1][1])]
        made = use(steps - 2, [*near[-2], *far[-1]])
        came = lax.optimization_barrier((*came, *made))[:2]
        far.append(came)
        use(steps - 1, [*near[-1], *far[-1]])
        return [a for pieces in zip(near, far) for both in pieces for a in both]

    me = lax.axis_index("path").astype(jnp.int32)
    where = jnp.concatenate([me[None], module_table.reshape(-1)])
    away = list(range(n_path))[::-1]
    far_away = [d for d in away if d > 1]
    first, second = far_away
    acts, slopes, own, peer, ahead, last_far, passed = [], [], [], [], [], [], [None, None]

    def run_forward(k, pieces):
        after = acts[-1:]
        if k == steps - 1:
            ahead.append(add_rows(peer[2][1], ahead[0]))
            after += ahead[-1:]
            last_far.extend(pieces[2:])
        types = (F32, BF16 if k == 1 else F32, BF16, BF16)
        act, slope, *parts = forward(pieces, weights, in_scale, out_scale, types, after)
        acts.append(act)
        slopes.append(slope)
        own.append(parts[:2])
        peer.append(parts[2:])
        if k == 1:
            ahead.append(ring(peer[1][1]))
            passed[1] = ring(own[1][1])
        if k == 0:
            send_base(1, [act])
        return [act, *({1: [base[0, first], sent[-1]], 2: [base[1, first]]}.get(k, []))]

    x_halves = [inputs[0, :half], inputs[0, half:]]
    base, sent = {}, []

    def send_base(d, after):
        made = base_rows(where, master, momentum, d, d == 1, after)
        sent.extend(made)
        for level in range(weights.shape[1]):
            base[level, d] = cross(made[level], d) if len(made) > level else base[0, d]

    for d in far_away:
        send_base(d, x_halves)
    x_all = gather(x_halves, run_forward, sent[:])

    wide = lambda a: a.astype(F32)
    for k in list(range(1, steps)) + [0]:
        for h in (0, 1):
            if (k, h) == (1, 1):
                continue
            out = peer[k][h]
            if (k, h) == (2, 1):
                out = ahead[-1]
            if k == steps - 2:
                out, *_ = lax.optimization_barrier((out, *last_far))
            came = swap(out)
            if 0 < k < steps - 1:
                pinned = [passed[1], base[0, second]] if (k, h) == (2, 0) else []
                came, *_ = lax.optimization_barrier((came, acts[k + 1], *pinned))
            total_rows = own[k][h] + wide(came)
            if passed[h] is not None:
                total_rows = total_rows + wide(passed[h])
            if k == 0:
                passed[h] = total_rows
                continue
            total_rows = total_rows.astype(BF16)
            if (k, h) == (steps - 1, 1):
                total_rows, *_ = lax.optimization_barrier((total_rows, base[0, 1], base[1, second]))
            if (k, h) == (steps - 1, 0):
                *peer[0], total_rows = lax.optimization_barrier((*peer[0], total_rows))
            passed[h] = ring(total_rows)
    grad = []
    for h, mine in enumerate(passed):
        part = slice(h * half, (h + 1) * half)
        keep = (token_ids[0, part] >= SPECIAL).astype(F32)
        residual = wide(inputs[0, part]) + mine - wide(targets[0, part])
        grad.append((keep[:, None] * residual / total).astype(BF16))

    pre_grads = []

    def run_backward(k, pieces):
        if k < steps - 1:
            after = pre_grads[-1:]
            pre_grads.append(backward(pieces, weights, slopes[k], out_scale, after))
        return pre_grads[-1:]

    g_all = gather(grad, run_backward, [])
    sides = {
        0: (INNER_LR * in_scale, pre_grads, x_all),
        1: (INNER_LR * out_scale, acts, g_all),
    }
    fresh, deltas, outer = [None], {}, [master, momentum]

    def rows(level, d):
        use = outer if d == 0 else None
        copied = (base.get((level, d)), fresh[0], weights.shape)
        out = module_rows(where, level, d, *sides[level], master.shape[3], d > 0, *copied, outer=use)
        if d:
            deltas[level, d] = cross(out[0], d)
            fresh[0] = out[1]
        else:
            fresh[0], *outer[2:] = out
        return out[0]

    made = rows(1, second)
    pre_grads.append(
        backward(g_all[-4:], weights, slopes[-1], out_scale, [*pre_grads[-1:], made])
    )
    rows(0, second)
    for d in (1, first, 0):
        for level in (1, 0):
            rows(level, d)
    for d in (second, 1, first):
        for level in (1, 0):
            outer[2:] = outer_rows(where, deltas[level, d], level, d, outer)
    new_master, new_momentum = outer[2:]
    return (
        jnp.swapaxes(fresh[0], 2, 3),
        jnp.swapaxes(new_master, 2, 3),
        jnp.swapaxes(new_momentum, 2, 3),
    )


def solution(mesh):
    in_specs = (
        P("path", "fsdp", None),
        P("path", "fsdp", None),
        P("path", "fsdp"),
        P(),
        P("path", None, None, "fsdp"),
        P(None, None, "path", "fsdp"),
        P(None, None, "path", "fsdp"),
    )
    out_specs = (
        P("path", None, None, "fsdp"),
        P(None, None, "path", "fsdp"),
        P(None, None, "path", "fsdp"),
    )
    shape = mesh.shape

    def step(*args):
        paths, pieces = shape["path"], shape["fsdp"]
        one_each = paths == args[5].shape[1] and paths & (paths - 1) == 0
        body = one_path_per_module if one_each and pieces % 2 == 0 and pieces > 5 else any_table
        return run(body)(*args)

    def run(body):
        return jax.shard_map(
            body, mesh=mesh, in_specs=in_specs, out_specs=out_specs, check_vma=False
        )

    return step
```

```python
import jax
import jax.numpy as jnp
from jax import lax
from jax.experimental import pallas as pl
from jax.experimental.pallas import tpu as pltpu
from jax.sharding import PartitionSpec as P

SPECIAL = 256


INNER_LR = 4096.0
OUTER_LR = 0.7
MOMENT = 0.9


def any_table(inputs, targets, token_ids, module_table, path_weights, master, momentum):
    x_local = inputs[0]
    w_in = path_weights[0, 0]
    w_out = path_weights[0, 1]
    width = w_in.shape[0]
    hidden_all = w_in.shape[1] * lax.axis_size("fsdp")
    out_scale = hidden_all ** (-0.5)
    x_full = lax.all_gather(x_local, "fsdp", axis=0, tiled=True)
    total = x_full.shape[0]
    pre = jnp.dot(x_full, w_in, preferred_element_type=jnp.float32) * width ** (-0.5)
    sig = jax.nn.sigmoid(pre)
    act = (pre * sig).astype(jnp.bfloat16)
    rows = act
    mine = lax.psum_scatter(
        (
            lax.dot_general(
                rows, w_out, (((1,), (1,)), ((), ())), preferred_element_type=jnp.float32
            )
            * out_scale
        ).astype(jnp.bfloat16),
        "fsdp",
        scatter_dimension=0,
        tiled=True,
    ).astype(jnp.float32)
    keep = (token_ids[0] >= SPECIAL).astype(jnp.float32)
    residual = x_local.astype(jnp.float32) + mine - targets[0].astype(jnp.float32)
    grad_mine = (keep[:, None] * residual / total).astype(jnp.bfloat16)
    piece = lax.all_gather(grad_mine, "fsdp", axis=0, tiled=True)
    rows = jnp.dot(piece, w_out, preferred_element_type=jnp.float32) * out_scale
    weight_acc = lax.dot_general(
        piece, act, (((0,), (0,)), ((), ())), preferred_element_type=jnp.float32
    )
    grad_out = weight_acc * out_scale
    pre_grad = (rows * sig * (1.0 + pre * (1.0 - sig))).astype(jnp.bfloat16)
    delta_out = INNER_LR * grad_out
    grad_in = lax.dot_general(
        x_full, pre_grad, (((0,), (0,)), ((), ())), preferred_element_type=jnp.float32
    ) * width ** (-0.5)
    stacked = jnp.stack([INNER_LR * grad_in, delta_out])[:, None]
    arrived = lax.all_to_all(
        stacked.astype(jnp.bfloat16), "path", split_axis=2, concat_axis=1, tiled=True
    ).astype(stacked.dtype)
    modules = master.shape[1]
    labels = jnp.arange(modules, dtype=jnp.int32)
    pick = (module_table.T[:, None, :] == labels[None, :, None]).astype(jnp.float32)
    counts = jnp.sum(pick, axis=2)
    sums = jnp.einsum("lmq,lqrc->lmrc", pick, arrived, precision=lax.Precision.HIGHEST)
    average = sums / counts[:, :, None, None]
    new_momentum = MOMENT * momentum + average
    new_master = master - OUTER_LR * (average + MOMENT * new_momentum)
    route = jnp.transpose(pick, (0, 2, 1)).astype(jnp.bfloat16)
    outgoing = jnp.einsum(
        "lqm,lmrc->lqrc", route, new_master.astype(jnp.bfloat16), preferred_element_type=jnp.float32
    ).astype(jnp.bfloat16)
    returned = lax.all_to_all(outgoing, "path", split_axis=1, concat_axis=2, tiled=True)
    new_weights = jnp.transpose(returned, (1, 0, 2, 3))
    return (new_weights, new_master, new_momentum)


MIB = 1024 * 1024
LANES = 1024
F32, BF16 = jnp.float32, jnp.bfloat16
NT = (((1,), (1,)), ((), ()))


def params(steps, room):
    return pltpu.CompilerParams(
        vmem_limit_bytes=room * MIB, dimension_semantics=("arbitrary",) * steps
    )


def cost(flops, moved):
    return pl.CostEstimate(flops=1, bytes_accessed=1, transcendentals=0)


def whole(shape):
    return pl.BlockSpec(shape, lambda *_: (0,) * len(shape))


def forward(pieces, weights, in_scale, out_scale, types, after):
    half, width = pieces[0].shape
    hidden = weights.shape[2]
    n, tokens = len(pieces), len(pieces) * half
    tiles = width // LANES

    def kernel(*refs):
        w_in, w_out = refs[n : n + 2]
        act_ref, slope_ref, *parts, pre_ref, flat_ref = refs[n + 2 + len(after) :]
        step = pl.program_id(0)

        @pl.when(step < tiles)
        def _():
            x = jnp.concatenate([ref[...] for ref in refs[:n]], axis=0)
            part = lax.dot_general(w_in[0, 0], x, NT, preferred_element_type=F32)

            @pl.when(step == 0)
            def _():
                pre_ref[...] = part

            @pl.when(step > 0)
            def _():
                pre_ref[...] += part

        @pl.when(step == tiles - 1)
        def _():
            pre = pre_ref[...] * in_scale
            sig = jax.nn.sigmoid(pre)
            act = pre * sig
            act_ref[...] = act.astype(BF16)
            flat_ref[...] = act.T.astype(BF16)
            slope_ref[...] = sig * (1.0 + pre * (1.0 - sig))

        @pl.when(step >= tiles)
        def _():
            part = jnp.dot(flat_ref[...], w_out[0, 0], preferred_element_type=F32) * out_scale
            for k, ref in enumerate(parts):
                ref[...] = part[k * half : (k + 1) * half].astype(ref.dtype)

    first = lambda i: (0, jnp.minimum(i, tiles - 1))
    last = lambda i: (0, jnp.maximum(i - tiles, 0))
    return pl.pallas_call(
        kernel,
        grid=(2 * tiles,),
        in_specs=[
            *[pl.BlockSpec((half, LANES), first)] * n,
            pl.BlockSpec((1, 1, hidden, LANES), lambda i: (0, 0) + first(i)),
            pl.BlockSpec((1, 1, hidden, LANES), lambda i: (0, 1) + last(i)),
        ]
        + [pl.BlockSpec(memory_space=pl.ANY)] * len(after),
        out_specs=[
            whole((hidden, tokens)),
            whole((hidden, tokens)),
            *[pl.BlockSpec((half, LANES), last)] * n,
        ],
        out_shape=[
            jax.ShapeDtypeStruct((hidden, tokens), BF16),
            jax.ShapeDtypeStruct((hidden, tokens), F32),
            *[jax.ShapeDtypeStruct((half, width), kind) for kind in types],
        ],
        scratch_shapes=[pltpu.VMEM((hidden, tokens), F32), pltpu.VMEM((tokens, hidden), BF16)],
        compiler_params=params(1, 18),
        cost_estimate=cost(4 * tokens * width * hidden, 4 * width * hidden + 10 * tokens * width),
        name="forward",
    )(*pieces, weights, weights, *after)


def backward(pieces, weights, slope, out_scale, after):
    half, width = pieces[0].shape
    hidden, tokens = slope.shape
    n = len(pieces)
    tiles = width // LANES

    def kernel(*refs):
        w_out, slope_ref = refs[n : n + 2]
        out_ref, sum_ref = refs[n + 2 + len(after) :]
        step = pl.program_id(0)
        g = jnp.concatenate([ref[...] for ref in refs[:n]], axis=0)
        part = lax.dot_general(w_out[0, 0], g, NT, preferred_element_type=F32)

        @pl.when(step == 0)
        def _():
            sum_ref[...] = part

        @pl.when(step > 0)
        def _():
            sum_ref[...] += part

        @pl.when(step == tiles - 1)
        def _():
            out_ref[...] = (sum_ref[...] * out_scale * slope_ref[...]).astype(BF16)

    return pl.pallas_call(
        kernel,
        grid=(tiles,),
        in_specs=[
            *[pl.BlockSpec((half, LANES), lambda i: (0, i))] * n,
            pl.BlockSpec((1, 1, hidden, LANES), lambda i: (0, 1, 0, i)),
            whole((hidden, tokens)),
        ]
        + [pl.BlockSpec(memory_space=pl.ANY)] * len(after),
        out_specs=whole((hidden, tokens)),
        out_shape=jax.ShapeDtypeStruct((hidden, tokens), BF16),
        scratch_shapes=[pltpu.VMEM((hidden, tokens), F32)],
        compiler_params=params(1, 12),
        cost_estimate=cost(2 * tokens * width * hidden, 2 * width * hidden + 2 * tokens * width),
        name="backward",
    )(*pieces, weights, slope, *after)


def untouched(arrays):
    return [pl.BlockSpec(memory_space=pl.ANY)] * len(arrays)


def add_rows(a, b):
    def kernel(a_ref, b_ref, out_ref):
        out_ref[...] = (a_ref[...].astype(F32) + b_ref[...].astype(F32)).astype(out_ref.dtype)

    return pl.pallas_call(
        kernel,
        out_shape=jax.ShapeDtypeStruct(a.shape, a.dtype),
        compiler_params=pltpu.CompilerParams(vmem_limit_bytes=4 * MIB),
        cost_estimate=cost(a.size, 6 * a.size),
        name="add_rows",
    )(a, b)


def base_rows(where, master, momentum, d, together, after):
    levels, _, hidden, block = master.shape

    def kernel(_, master_ref, momentum_ref, *refs):
        value = master_ref[0, 0] - (OUTER_LR * MOMENT * MOMENT) * momentum_ref[0, 0]
        outs = refs[len(after) :]
        if together:
            outs[0][0] = value.astype(BF16)
            return
        for level, out_ref in enumerate(outs):

            @pl.when(pl.program_id(0) == level)
            def _(out_ref=out_ref):
                out_ref[...] = value.astype(BF16)

    source = pl.BlockSpec(
        (1, 1, hidden, block), lambda l, s: (l, s[1 + (s[0] ^ d) * levels + l], 0, 0)
    )
    return pl.pallas_call(
        kernel,
        grid_spec=pltpu.PrefetchScalarGridSpec(
            num_scalar_prefetch=1,
            grid=(levels,),
            in_specs=[source, source] + untouched(after),
            out_specs=[pl.BlockSpec((1, hidden, block), lambda l, s: (l, 0, 0))]
            if together
            else [whole((hidden, block))] * levels,
        ),
        out_shape=[jax.ShapeDtypeStruct((levels, hidden, block), BF16)]
        if together
        else [jax.ShapeDtypeStruct((hidden, block), BF16)] * levels,
        compiler_params=params(1, 42),
        cost_estimate=cost(3 * levels * hidden * block, 10 * levels * hidden * block),
        name="base_rows",
    )(where, master, momentum, *after)


def module_rows(
    where, level, d, scale, lefts, rights, block, send=False, base=None, fresh=None, copy_shape=None, outer=None, extra=None, after=()
):
    rows, wide = rights[0].shape
    hidden, tokens = lefts[0].shape
    tile = hidden if outer is None else hidden // 2
    n_left, n_right = len(lefts), len(rights)
    operands = [*lefts, *rights]
    in_specs = [pl.BlockSpec((tile, tokens), lambda i, s: (i, 0))] * n_left
    in_specs += [pl.BlockSpec((rows, block), lambda i, s: (0, s[0] ^ d if wide > block else 0))] * n_right
    if extra is not None:
        operands.append(extra)
        in_specs.append(pl.BlockSpec((tile, block), lambda i, s: (i, 0)))
    out_specs, out_shape, aliases = [], [], {}
    if send:
        out_specs.append(pl.BlockSpec((tile, block), lambda i, s: (i, 0)))
        out_shape.append(jax.ShapeDtypeStruct((hidden, block), BF16))
    if base is not None:
        operands.append(base)
        if base.ndim == 3:
            in_specs.append(pl.BlockSpec((1, tile, block), lambda i, s: (level, i, 0)))
        else:
            in_specs.append(pl.BlockSpec((tile, block), lambda i, s: (i, 0)))
    if copy_shape is not None:
        if fresh is not None:
            operands.append(fresh)
            in_specs += untouched([fresh])
            aliases[len(operands)] = len(out_shape)
        out_specs.append(pl.BlockSpec((1, 1, tile, block), lambda i, s: (0, level, i, s[0] ^ d)))
        out_shape.append(jax.ShapeDtypeStruct(copy_shape, BF16))
    if outer is not None:
        master, momentum, *state = outer
        levels = master.shape[0]
        place = pl.BlockSpec(
            (1, 1, tile, block), lambda i, s: (level, s[1 + (s[0] ^ d) * levels + level], i, 0)
        )
        operands += [master, momentum, *state]
        in_specs += [place, place] + untouched(state)
        for k in range(len(state)):
            aliases[len(operands) - 1 + k] = len(out_shape) + k
        out_specs += [place, place]
        out_shape += [jax.ShapeDtypeStruct(master.shape, F32)] * 2
    n_in = len(operands) + len(after)

    def kernel(_, *refs):
        ins, outs = list(refs[:n_in]), list(refs[n_in:])
        left = jnp.concatenate([ref[...] for ref in ins[:n_left]], axis=1)
        right = jnp.concatenate([ref[...] for ref in ins[n_left : n_left + n_right]], axis=0)
        rest = ins[n_left + n_right :]
        delta = jnp.dot(left, right, preferred_element_type=F32) * scale
        if extra is not None:
            delta = delta + rest.pop(0)[...].astype(F32)
        if send:
            outs.pop(0)[...] = delta.astype(BF16)
        if base is not None:
            start = rest.pop(0)[...].astype(F32).reshape(tile, block)
            outs.pop(0)[0, 0] = (start - (OUTER_LR * (1.0 + MOMENT)) * delta).astype(BF16)
        if fresh is not None:
            rest.pop(0)
        if outer is not None:
            nesterov(delta, *rest[:2], *outs[-2:])
            if copy_shape is not None:
                outs[0][0, 0] = outs[-2][0, 0].astype(BF16)

    return pl.pallas_call(
        kernel,
        grid_spec=pltpu.PrefetchScalarGridSpec(
            num_scalar_prefetch=1,
            grid=(hidden // tile,),
            in_specs=in_specs + untouched(after),
            out_specs=out_specs,
        ),
        out_shape=out_shape,
        input_output_aliases=aliases,
        compiler_params=params(1, 24 if outer is None else 48),
        cost_estimate=cost(2 * hidden * block * rows * n_right, 2 * rows * n_right * (hidden + block)),
        name="module_rows",
    )(where, *operands, *after)


def take_columns(where, pieces, block, d):
    rows, n = pieces[0].shape[0], len(pieces)

    def kernel(_, *refs):
        refs[-1][...] = jnp.concatenate([ref[...] for ref in refs[:n]], axis=0)

    return pl.pallas_call(
        kernel,
        grid_spec=pltpu.PrefetchScalarGridSpec(
            num_scalar_prefetch=1,
            grid=(1,),
            in_specs=[pl.BlockSpec((rows, block), lambda i, s: (0, s[0] ^ d))] * n,
            out_specs=whole((n * rows, block)),
        ),
        out_shape=jax.ShapeDtypeStruct((n * rows, block), BF16),
        compiler_params=params(1, 4),
        cost_estimate=cost(0, 4 * n * rows * block),
        name="take_columns",
    )(where, *pieces)


def nesterov(average, master_ref, momentum_ref, new_master, new_momentum):
    moved = MOMENT * momentum_ref[0, 0] + average
    new_momentum[0, 0] = moved
    new_master[0, 0] = master_ref[0, 0] - OUTER_LR * (average + MOMENT * moved)


def outer_rows(where, deltas, levels, d, outer):
    master, momentum, *state = outer
    n_levels, _, hidden, block = master.shape
    tile, n = hidden // 2, len(deltas)

    def kernel(_, *refs):
        step = pl.program_id(0)
        average = refs[0][...].astype(F32)
        for k in range(1, n):
            average = jnp.where(step < 2 * k, average, refs[k][...].astype(F32))
        nesterov(average, *refs[n : n + 2], *refs[-2:])

    def level_of(i):
        return levels[0] + (levels[-1] - levels[0]) * (i // 2)

    place = pl.BlockSpec(
        (1, 1, tile, block),
        lambda i, s: (level_of(i), s[1 + (s[0] ^ d) * n_levels + level_of(i)], i % 2, 0),
    )
    rows = [
        pl.BlockSpec((tile, block), lambda i, s, k=k: (jnp.clip(i - 2 * k, 0, 1), 0)) for k in range(n)
    ]
    return pl.pallas_call(
        kernel,
        grid_spec=pltpu.PrefetchScalarGridSpec(
            num_scalar_prefetch=1,
            grid=(2 * n,),
            in_specs=rows + [place, place] + untouched(state),
            out_specs=[place, place],
        ),
        out_shape=[jax.ShapeDtypeStruct(master.shape, F32)] * 2,
        input_output_aliases={n + 3: 0, n + 4: 1} if state else {},
        compiler_params=params(1, 48),
        cost_estimate=cost(6 * hidden * block, 18 * hidden * block),
        name="outer_rows",
    )(where, *deltas, master, momentum, *state)


def one_path_per_module(inputs, targets, token_ids, module_table, path_weights, master, momentum):
    n_path, n_fsdp = lax.axis_size("path"), lax.axis_size("fsdp")
    steps = n_fsdp // 2
    weights = jnp.swapaxes(path_weights, 2, 3)
    master = jnp.swapaxes(master, 2, 3)
    momentum = jnp.swapaxes(momentum, 2, 3)
    width, hidden = path_weights.shape[2:]
    in_scale = width ** (-0.5)
    out_scale = (hidden * n_fsdp) ** (-0.5)
    total = inputs.shape[1] * n_fsdp

    def ring(a):
        return lax.ppermute(a, "fsdp", [(i, (i + 2) % n_fsdp) for i in range(n_fsdp)])

    def swap(a):
        return lax.ppermute(a, "fsdp", [(i, i ^ 1) for i in range(n_fsdp)])

    def cross(a, d):
        return lax.ppermute(a, "path", [(i, i ^ d) for i in range(n_path)])

    half = inputs.shape[1] // 2

    def gather(halves, use, made):
        near, far = [halves], []
        for k in range(steps - 1):
            got, came = [], []
            for h in (0, 1):
                got.append(ring(near[k][h]))
                came.append(swap(near[k][h]))
            if k:
                made = use(k - 1, [*near[k - 1], *far[k - 1]])
            for h in (0, 1):
                got[h], came[h], *_ = lax.optimization_barrier((got[h], came[h], *made))
            near.append(got)
            far.append(came)
        came = [swap(near[-1][0]), ring(far[-1][1])]
        made = use(steps - 2, [*near[-2], *far[-1]])
        came = lax.optimization_barrier((*came, *made))[:2]
        far.append(came)
        use(steps - 1, [*near[-1], *far[-1]])
        return [a for pieces in zip(near, far) for both in pieces for a in both]

    me = lax.axis_index("path").astype(jnp.int32)
    where = jnp.concatenate([me[None], module_table.reshape(-1)])
    away = list(range(n_path))[::-1]
    far_away = [d for d in away if d > 1]
    first, second = far_away
    acts, slopes, own, peer, ahead, last_far, passed = [], [], [], [], [], [], [None, None]

    def run_forward(k, pieces):
        after = acts[-1:]
        if k == steps - 1:
            ahead.append(add_rows(peer[2][1], ahead[0]))
            after += ahead[-1:]
            last_far.extend(pieces[2:])
        types = (F32, BF16 if k == 1 else F32, BF16, BF16)
        act, slope, *parts = forward(pieces, weights, in_scale, out_scale, types, after)
        acts.append(act)
        slopes.append(slope)
        own.append(parts[:2])
        peer.append(parts[2:])
        if k == 1:
            ahead.append(ring(peer[1][1]))
            passed[1] = ring(own[1][1])
        if k == 0:
            send_base(1, [act])
        return [act, *({1: [base[0, first], sent[-1]], 2: [base[1, first]]}.get(k, []))]

    x_halves = [inputs[0, :half], inputs[0, half:]]
    base, sent = {}, []

    def send_base(d, after):
        made = base_rows(where, master, momentum, d, d == 1, after)
        sent.extend(made)
        for level in range(weights.shape[1]):
            base[level, d] = cross(made[level], d) if len(made) > level else base[0, d]

    for d in far_away:
        send_base(d, x_halves)
    x_all = gather(x_halves, run_forward, sent[:])

    wide = lambda a: a.astype(F32)
    for k in list(range(1, steps)) + [0]:
        for h in (0, 1):
            if (k, h) == (1, 1):
                continue
            out = peer[k][h]
            if (k, h) == (2, 1):
                out = ahead[-1]
            if k == steps - 2:
                out, *_ = lax.optimization_barrier((out, *last_far))
            came = swap(out)
            if 0 < k < steps - 1:
                pinned = [passed[1], base[0, second]] if (k, h) == (2, 0) else []
                came, *_ = lax.optimization_barrier((came, acts[k + 1], *pinned))
            total_rows = own[k][h] + wide(came)
            if passed[h] is not None:
                total_rows = total_rows + wide(passed[h])
            if k == 0:
                passed[h] = total_rows
                continue
            total_rows = total_rows.astype(BF16)
            if (k, h) == (steps - 1, 1):
                total_rows, *_ = lax.optimization_barrier((total_rows, base[0, 1], base[1, second]))
            if (k, h) == (steps - 1, 0):
                *peer[0], total_rows = lax.optimization_barrier((*peer[0], total_rows))
            passed[h] = ring(total_rows)
    grad = []
    for h, mine in enumerate(passed):
        part = slice(h * half, (h + 1) * half)
        keep = (token_ids[0, part] >= SPECIAL).astype(F32)
        residual = wide(inputs[0, part]) + mine - wide(targets[0, part])
        grad.append((keep[:, None] * residual / total).astype(BF16))

    pre_grads = []

    out_side, block = INNER_LR * out_scale, master.shape[3]
    last_act = cross(acts[-1], second)
    g_parts, early = [], []

    def run_backward(k, pieces):
        g_parts.extend(pieces)
        if k == steps - 1:
            return []
        pre_grads.append(backward(pieces, weights, slopes[k], out_scale, pre_grads[-1:]))
        made = pre_grads[-1:]
        if k == 0:
            made = made + [last_act]
        if k == steps - 2:
            early.extend(module_rows(where, 1, second, out_side, acts[:-1], g_parts[:], block, True))
            made = made + early
        return made

    g_all = gather(grad, run_backward, [])
    sides = {
        0: (INNER_LR * in_scale, pre_grads, x_all),
        1: (out_side, acts, g_all),
    }
    fresh, deltas, outer = [None], {}, [master, momentum]

    def rows(level, d, after=()):
        use = outer if d == 0 else None
        send = d > 0 and (level, d) != (1, second)
        copied = (base.get((level, d)), fresh[0], weights.shape)
        out = module_rows(
            where, level, d, *sides[level], block, send, *copied, outer=use, after=after
        )
        if send:
            deltas[level, d] = cross(out[0], d)
        if d:
            fresh[0] = out[-1]
        else:
            fresh[0], *outer[2:] = out

    early_there = cross(early[0], second)
    columns = take_columns(where, g_all[-4:], block, second)
    columns_there = cross(columns, second)
    pre_grads.append(
        backward(g_all[-4:], weights, slopes[-1], out_scale, [*pre_grads[-1:], columns])
    )
    rows(0, second)
    for key in [(1, first), (1, 1), (0, 1), (0, first), (1, second), (1, 0), (0, 0)]:
        rows(*key, [early_there] if key == (0, 1) else [])
    outer[2:] = module_rows(
        where, 1, second, out_side, [last_act], [columns_there], block, outer=outer, extra=early_there
    )
    for levels, d in [((0,), second), ((1,), first), ((1, 0), 1), ((0,), first)]:
        outer[2:] = outer_rows(where, [deltas[level, d] for level in levels], levels, d, outer)
    new_master, new_momentum = outer[2:]
    return (
        jnp.swapaxes(fresh[0], 2, 3),
        jnp.swapaxes(new_master, 2, 3),
        jnp.swapaxes(new_momentum, 2, 3),
    )


def solution(mesh):
    in_specs = (
        P("path", "fsdp", None),
        P("path", "fsdp", None),
        P("path", "fsdp"),
        P(),
        P("path", None, None, "fsdp"),
        P(None, None, "path", "fsdp"),
        P(None, None, "path", "fsdp"),
    )
    out_specs = (
        P("path", None, None, "fsdp"),
        P(None, None, "path", "fsdp"),
        P(None, None, "path", "fsdp"),
    )
    shape = mesh.shape

    def step(*args):
        paths, pieces = shape["path"], shape["fsdp"]
        one_each = paths == args[5].shape[1] and paths & (paths - 1) == 0
        body = one_path_per_module if one_each and pieces % 2 == 0 and pieces > 5 else any_table
        return run(body)(*args)

    def run(body):
        return jax.shard_map(
            body, mesh=mesh, in_specs=in_specs, out_specs=out_specs, check_vma=False
        )

    return step
```
